256 devices in a mesh: kv: 128 (over y_lo, z, x, core), occ: 2 (over y_hi).
Axes of the slice: x: 4, y: 4 (y_hi: 2, y_lo: 2; y = y_hi * 2 + y_lo), z: 8, core: 2. Of those that a mesh axis runs over, the one named last changes fastest.
Arguments:
- factors: bfloat16 [128, 6, 128, 1024], P('kv', 'occ'), may hold values from -1.078125 to 1.078125
- occ_energy: float32 [128, 6], replicated, may hold values from -2 to -0.5
- vir_energy: float32 [128, 128], replicated, may hold values from 0.5 to 3
- partners: int32 [1, 128], replicated, may hold values from 0 to 127, as said below
Outputs:
- density: float32 [128, 6, 128, 1024], P('kv', 'occ')
The draws below stay inside these ranges and needn't reach their ends.
Inputs may be any that keep to these rules, and one draw needn't show every extreme that they name: `partners`: row p maps each momentum k to k XOR m_p for one nonzero m_p per row; the 1 values m_p differ, so every row is an involution without fixed points.
All inputs are finite; a program needn't handle non-finite values.
Results may differ from the reference program's by a relative error of at most 0.0065.
Values may be sent and summed in bfloat16 or wider, within the bound.
No kernel may reach another device: no remote copies, remote signals or barrier semaphores. Data moves between devices by JAX's collectives and lax.ppermute only.
A program may use at most 64 MiB of HBM per device.

```python
import jax
import jax.numpy as jnp
from jax import lax

NVIR = 128
NAUX = 1024
PAIRS = 1
NOCC = 6
NK = 128


def draw_partners(key, part):
    key = jax.random.fold_in(key, 11)
    picks = jax.random.permutation(key, NK - 1)[:PAIRS] + 1
    return jnp.bitwise_xor(jnp.arange(NK, dtype=jnp.int32)[None, :], picks.astype(jnp.int32)[:, None])


def levels(stream_key, shape, pieces, least, top_value):
    def one(position, shards_of):
        steps = jax.random.uniform(jax.random.fold_in(jax.random.fold_in(stream_key, 6), position), (shards_of,), jnp.float32, least / len(pieces), top_value / len(pieces))
        return jnp.repeat(jnp.exp(steps), shape[position] // shards_of).reshape((-1,) + (1,) * (len(shape) - position - 1))

    loudness = one(*pieces[0])
    for cut in pieces[1:]:
        loudness = loudness * one(*cut)
    return loudness


def bell_draw(own_key, shape, scale, limit, shards=(), kind=jnp.bfloat16):
    result = jax.random.normal(own_key, shape, jnp.float32) * scale
    if len(shards) > 0:
        result = levels(own_key, shape, shards, -0.22, 0.18) * result
    return jnp.clip(result, min=-limit, max=limit).astype(kind)


def setup_inputs(seed: int = 0) -> dict:
    key_of = jax.random.split(jax.random.key(seed), 5)
    factors = bell_draw(key_of[0], (NK, NOCC, NVIR, NAUX), 0.18, 1.078125, ((0, 128), (1, 2)))
    occ_energy = jnp.clip(jax.random.uniform(key_of[1], (NK, NOCC), jnp.float32, -2.0, -0.5), -2.0, -0.5)
    vir_energy = jnp.clip(jax.random.uniform(key_of[2], (NK, NVIR), jnp.float32, 0.5, 3.0), 0.5, 3.0)
    partners = draw_partners(jax.random.fold_in(key_of[4], 71), 0)
    return dict(factors=factors, occ_energy=occ_energy, vir_energy=vir_energy, partners=partners)


def reference(factors, occ_energy, vir_energy, partners):
    def one_momentum(momentum):
        own_rows = factors[momentum].reshape(NOCC * NVIR, NAUX)
        own_occ = occ_energy[momentum]
        own_vir = vir_energy[momentum]
        density = jnp.zeros((NOCC * NVIR, NAUX), jnp.float32)
        for pair_index in range(PAIRS):
            partner = partners[pair_index, momentum]
            partner_rows = factors[partner].reshape(NOCC * NVIR, NAUX)
            far_occ = occ_energy[partner]
            far_vir = vir_energy[partner]
            direct_den = own_occ[:, None, None, None] + far_occ[None, None, :, None] - own_vir[None, :, None, None] - far_vir[None, None, None, :]
            numer = jnp.dot(own_rows, partner_rows.T, preferred_element_type=jnp.float32).reshape(NOCC, NVIR, NOCC, NVIR)
            direct = (numer / direct_den).astype(jnp.bfloat16)
            swap_den = far_occ[:, None, None, None] + own_occ[None, None, :, None] - far_vir[None, :, None, None] - own_vir[None, None, None, :]
            swapped = jnp.dot(partner_rows, own_rows.T, preferred_element_type=jnp.float32).reshape(NOCC, NVIR, NOCC, NVIR)
            crossed = (swapped / swap_den).astype(jnp.bfloat16)
            exchanged = jnp.transpose(crossed, (2, 1, 0, 3))
            combined = (2.0 * direct.astype(jnp.float32) - exchanged.astype(jnp.float32)).astype(jnp.bfloat16)
            density = density + jnp.dot(combined.reshape(NOCC * NVIR, NOCC * NVIR), partner_rows, preferred_element_type=jnp.float32)
        return density.reshape(NOCC, NVIR, NAUX)

    return lax.map(one_momentum, jnp.arange(NK, dtype=jnp.int32))
```

```python
import functools

import jax
import jax.numpy as jnp
from jax import lax
from jax.experimental import pallas as pl
from jax.experimental.pallas import tpu as pltpu
from jax.sharding import PartitionSpec as P


def combine_kernel(where, occ, vir, own, *refs):
    blocks, out = refs[:-1], refs[-1]
    occ_dev, vir_count, _ = own.shape
    k, q, own_base, far_base = where[0], where[1], where[2], where[3]
    own_vir = jnp.transpose(jnp.broadcast_to(vir[pl.ds(k, 1), :], (vir_count, vir_count)))
    vir_sum = own_vir + vir[pl.ds(q, 1), :]
    own_rows = own[...].reshape(occ_dev * vir_count, -1)
    for step, block in enumerate(blocks):
        side, place = divmod(step, occ_dev)
        base = far_base if side else own_base
        far = block[...].reshape(vir_count, -1)
        numer = lax.dot_general(
            own_rows, far, (((1,), (1,)), ((), ())), preferred_element_type=jnp.float32
        )
        pieces = []
        for i in range(occ_dev):
            den = (occ[k, own_base + i] + occ[q, base + place]) - vir_sum
            direct = (numer[i * vir_count : (i + 1) * vir_count] / den).astype(jnp.bfloat16).astype(jnp.float32)
            pieces.append((2.0 * direct - jnp.transpose(direct)).astype(jnp.bfloat16))
        part = jnp.dot(jnp.concatenate(pieces, axis=0), far, preferred_element_type=jnp.float32)
        part = part.reshape(out.shape)
        if step == 0:
            out[...] = part
        else:
            out[...] += part


def combine(where, occ_energy, vir_energy, own, blocks):
    rows = own.shape[0] * own.shape[1]
    aux = own.shape[2]
    columns = len(blocks) * own.shape[1]
    vmem = pl.BlockSpec(memory_space=pltpu.VMEM)
    smem = pl.BlockSpec(memory_space=pltpu.SMEM)
    return pl.pallas_call(
        combine_kernel,
        out_shape=jax.ShapeDtypeStruct(own.shape, jnp.float32),
        in_specs=[smem, smem, vmem, vmem] + [vmem] * len(blocks),
        out_specs=vmem,
        compiler_params=pltpu.CompilerParams(vmem_limit_bytes=32 << 20),
        cost_estimate=pl.CostEstimate(
            flops=4 * rows * columns * aux, bytes_accessed=6 * rows * aux + 2 * columns * aux, transcendentals=0
        ),
    )(where, occ_energy, vir_energy, own, *blocks)


def hop(x, mask, side, kv_count, occ_groups):
    pairs = [
        (k * occ_groups + o, (k ^ mask) * occ_groups + (o ^ side))
        for k in range(kv_count)
        for o in range(occ_groups)
    ]
    return lax.ppermute(x, ("kv", "occ"), pairs)


def turn(own, kv_count, occ_groups):
    return tuple(hop(own, 1, 0, kv_count, occ_groups))


def fetch(mask, kv_count, occ_groups, *pieces):
    top = kv_count // 2
    move = functools.partial(hop, kv_count=kv_count, occ_groups=occ_groups)
    near, far = [], []
    for piece in pieces:
        if mask & ~top:
            piece = move(piece, mask & ~top, 0)
        if mask & top:
            near.append(move(piece, top, 0))
            far.append(move(piece, top, 1))
        else:
            near.append(piece)
            far.append(move(piece, 0, 1))
    return tuple(near + far)


def shards(factors, occ_energy, vir_energy, partners):
    kv_count = lax.axis_size("kv")
    occ_groups = lax.axis_size("occ")
    k = lax.axis_index("kv")
    occ_block = lax.axis_index("occ")
    occ_dev = factors.shape[1]
    own = factors[0]
    mask = partners[0, 0]
    pieces = lax.cond(
        jnp.bitwise_and(mask, 1) == 1,
        functools.partial(turn, kv_count=kv_count, occ_groups=occ_groups),
        tuple,
        own,
    )
    branches = [functools.partial(fetch, m, kv_count, occ_groups) for m in range(0, kv_count, 2)]
    blocks = lax.switch(jnp.right_shift(mask, 1), branches, *pieces)
    where = jnp.stack([k, jnp.bitwise_xor(k, mask), occ_block * occ_dev, (1 - occ_block) * occ_dev]).astype(jnp.int32)
    return combine(where, occ_energy, vir_energy, own, blocks)[None]


def solution(mesh):
    placed = (P("kv", "occ", None, None), P(), P(), P())
    return jax.shard_map(
        shards, mesh=mesh, in_specs=placed, out_specs=P("kv", "occ", None, None), check_vma=False
    )
```

```python
import functools

import jax
import jax.numpy as jnp
from jax import lax
from jax.experimental import pallas as pl
from jax.experimental.pallas import tpu as pltpu
from jax.sharding import PartitionSpec as P


def combine_kernel(where, occ, vir, own, *refs):
    blocks, out = refs[:-1], refs[-1]
    occ_dev, vir_count, _ = own.shape
    k, q, own_base, far_base = where[0], where[1], where[2], where[3]
    own_vir = jnp.transpose(jnp.broadcast_to(vir[pl.ds(k, 1), :], (vir_count, vir_count)))
    vir_sum = own_vir + vir[pl.ds(q, 1), :]
    own_rows = own[...].reshape(occ_dev * vir_count, -1)
    for step in range(len(blocks) * occ_dev):
        side, place = divmod(step, occ_dev)
        base = far_base if side else own_base
        far = blocks[side][place]
        numer = lax.dot_general(
            own_rows, far, (((1,), (1,)), ((), ())), preferred_element_type=jnp.float32
        )
        pieces = []
        for i in range(occ_dev):
            den = (occ[k, own_base + i] + occ[q, base + place]) - vir_sum
            direct = (numer[i * vir_count : (i + 1) * vir_count] / den).astype(jnp.bfloat16).astype(jnp.float32)
            pieces.append((2.0 * direct - jnp.transpose(direct)).astype(jnp.bfloat16))
        part = jnp.dot(jnp.concatenate(pieces, axis=0), far, preferred_element_type=jnp.float32)
        part = part.reshape(out.shape)
        if step == 0:
            out[...] = part
        else:
            out[...] += part


def combine(where, occ_energy, vir_energy, own, blocks):
    rows = own.shape[0] * own.shape[1]
    aux = own.shape[2]
    columns = len(blocks) * rows
    vmem = pl.BlockSpec(memory_space=pltpu.VMEM)
    smem = pl.BlockSpec(memory_space=pltpu.SMEM)
    return pl.pallas_call(
        combine_kernel,
        out_shape=jax.ShapeDtypeStruct(own.shape, jnp.float32),
        in_specs=[smem, smem, vmem, vmem] + [vmem] * len(blocks),
        out_specs=vmem,
        compiler_params=pltpu.CompilerParams(vmem_limit_bytes=32 << 20),
        cost_estimate=pl.CostEstimate(
            flops=4 * rows * columns * aux, bytes_accessed=6 * rows * aux + 2 * columns * aux, transcendentals=0
        ),
    )(where, occ_energy, vir_energy, own, *blocks)


def hop(x, mask, side, kv_count, occ_groups):
    pairs = [
        (k * occ_groups + o, (k ^ mask) * occ_groups + (o ^ side))
        for k in range(kv_count)
        for o in range(occ_groups)
    ]
    return lax.ppermute(x, ("kv", "occ"), pairs)


def route(mask, kv_count, occ_groups, own):
    return hop(own, mask, 0, kv_count, occ_groups) if mask else own


def share(mask, kv_count, occ_groups, here):
    near = hop(here, mask, 0, kv_count, occ_groups) if mask else here
    return near, hop(here, mask, 1, kv_count, occ_groups)


def shards(factors, occ_energy, vir_energy, partners):
    kv_count = lax.axis_size("kv")
    occ_groups = lax.axis_size("occ")
    k = lax.axis_index("kv")
    occ_block = lax.axis_index("occ")
    occ_dev = factors.shape[1]
    own = factors[0]
    mask = partners[0, 0]
    top = kv_count // 2

    def routes(masks):
        return [functools.partial(route, m, kv_count, occ_groups) for m in masks]

    here = lax.switch(jnp.bitwise_and(mask, 1), routes((0, 1)), own)
    here = lax.switch(jnp.bitwise_and(mask, top - 1) >> 1, routes(range(0, top, 2)), here)
    shares = [functools.partial(share, m, kv_count, occ_groups) for m in (0, top)]
    near, far = lax.switch(jnp.bitwise_and(mask, top) // top, shares, here)
    where = jnp.stack([k, jnp.bitwise_xor(k, mask), occ_block * occ_dev, (1 - occ_block) * occ_dev]).astype(jnp.int32)
    return combine(where, occ_energy, vir_energy, own, (near, far))[None]


def solution(mesh):
    placed = (P("kv", "occ", None, None), P(), P(), P())
    return jax.shard_map(
        shards, mesh=mesh, in_specs=placed, out_specs=P("kv", "occ", None, None), check_vma=False
    )
```

```python
import functools

import jax
import jax.numpy as jnp
from jax import lax
from jax.experimental import pallas as pl
from jax.experimental.pallas import tpu as pltpu
from jax.sharding import PartitionSpec as P


GROUP = 2


def combine_kernel(where, occ, vir, own, near, far, out, rows, comb, result, in_sems, out_sems):
    occ_dev, vir_count, aux = own.shape
    half = occ_dev * vir_count
    k, q, own_base, far_base = where[0], where[1], where[2], where[3]
    loads = []
    for side, block in enumerate((near, far)):
        loads.append(pltpu.make_async_copy(block, rows.at[pl.ds(side * occ_dev, occ_dev)], in_sems.at[side]))
        loads[-1].start()
    own_vir = jnp.transpose(jnp.broadcast_to(vir[pl.ds(k, 1), :], (vir_count, vir_count)))
    vir_sum = own_vir + vir[pl.ds(q, 1), :]
    own_rows = own[...].reshape(half, aux)
    loads[0].wait()

    def mix(step, carry):
        @pl.when(step == occ_dev // GROUP)
        def _():
            loads[1].wait()

        other = rows[pl.ds(step * GROUP, GROUP)].reshape(GROUP * vir_count, aux)
        numer = lax.dot_general(
            own_rows, other, (((1,), (1,)), ((), ())), preferred_element_type=jnp.float32
        )
        for place in range(GROUP):
            j = step * GROUP + place
            far_occ = occ[q, j + jnp.where(j < occ_dev, own_base, far_base - occ_dev)]
            there = place * vir_count
            for i in range(occ_dev):
                here = i * vir_count
                den = (occ[k, own_base + i] + far_occ) - vir_sum
                tile = numer[here : here + vir_count, there : there + vir_count]
                direct = (tile / den).astype(jnp.bfloat16).astype(jnp.float32)
                mixed = (2.0 * direct - jnp.transpose(direct)).astype(jnp.bfloat16)
                comb[step, here : here + vir_count, there : there + vir_count] = mixed
        return carry

    steps = comb.shape[0]
    lax.fori_loop(0, steps, mix, 0)
    strips = out_sems.shape[0]
    wide = aux // strips

    def store(strip):
        cols = pl.ds(pl.multiple_of(strip * wide, wide), wide)
        return pltpu.make_async_copy(result.at[:, :, cols], out.at[:, :, cols], out_sems.at[strip])

    def fold(strip, carry):
        cols = pl.ds(pl.multiple_of(strip * wide, wide), wide)
        part = jnp.zeros((half, wide), jnp.float32)
        for step in range(steps):
            other = rows[step * GROUP : (step + 1) * GROUP, :, cols].reshape(GROUP * vir_count, wide)
            part += jnp.dot(comb[step], other, preferred_element_type=jnp.float32)
        result[:, :, cols] = part.reshape(occ_dev, vir_count, wide)
        store(strip).start()
        return carry

    lax.fori_loop(0, strips, fold, 0)
    for strip in range(strips):
        store(strip).wait()


def combine(where, occ_energy, vir_energy, own, near, far, strips=4):
    occ_dev, vir_count, aux = own.shape
    half = occ_dev * vir_count
    vmem = pl.BlockSpec(memory_space=pltpu.VMEM)
    smem = pl.BlockSpec(memory_space=pltpu.SMEM)
    anywhere = pl.BlockSpec(memory_space=pl.ANY)
    return pl.pallas_call(
        combine_kernel,
        out_shape=jax.ShapeDtypeStruct(own.shape, jnp.float32),
        in_specs=[smem, smem, vmem, vmem, anywhere, anywhere],
        out_specs=anywhere,
        scratch_shapes=[
            pltpu.VMEM((2 * occ_dev, vir_count, aux), own.dtype),
            pltpu.VMEM((2 * occ_dev // GROUP, half, GROUP * vir_count), own.dtype),
            pltpu.VMEM(own.shape, jnp.float32),
            pltpu.SemaphoreType.DMA((2,)),
            pltpu.SemaphoreType.DMA((strips,)),
        ],
        compiler_params=pltpu.CompilerParams(vmem_limit_bytes=24 << 20),
        cost_estimate=pl.CostEstimate(
            flops=8 * half * half * aux, bytes_accessed=10 * half * aux, transcendentals=0
        ),
    )(where, occ_energy, vir_energy, own, near, far)


def hop(x, mask, side, kv_count, occ_groups):
    pairs = [
        (k * occ_groups + o, (k ^ mask) * occ_groups + (o ^ side))
        for k in range(kv_count)
        for o in range(occ_groups)
    ]
    return lax.ppermute(x, ("kv", "occ"), pairs)


def route(mask, kv_count, occ_groups, own):
    return hop(own, mask, 0, kv_count, occ_groups) if mask else own


def share(mask, kv_count, occ_groups, here):
    top = kv_count // 2
    if mask & top and mask != top:
        here = hop(here, mask - top, 0, kv_count, occ_groups)
        mask = top
    near = hop(here, mask, 0, kv_count, occ_groups) if mask else here
    return near, hop(here, mask, 1, kv_count, occ_groups)


def choose(index, branches, operand):
    if len(branches) <= 16:
        return lax.switch(index, branches, operand)
    half = len(branches) // 2
    return lax.cond(
        index < half,
        lambda x: choose(index, branches[:half], x),
        lambda x: choose(index - half, branches[half:], x),
        operand,
    )


def shards(factors, occ_energy, vir_energy, partners):
    kv_count = lax.axis_size("kv")
    occ_groups = lax.axis_size("occ")
    k = lax.axis_index("kv")
    occ_block = lax.axis_index("occ")
    occ_dev = factors.shape[1]
    own = factors[0]
    mask = partners[0, 0]
    top = kv_count // 2

    def routes(masks):
        return [functools.partial(route, m, kv_count, occ_groups) for m in masks]

    along = jnp.right_shift(jnp.bitwise_and(mask, top - 1), 1)
    here = choose(along, routes(range(0, top, 2)), own)
    shares = [functools.partial(share, m, kv_count, occ_groups) for m in (0, 1, top, top + 1)]
    last = jnp.bitwise_and(mask, 1) + 2 * jnp.right_shift(mask, kv_count.bit_length() - 2)
    near, far = lax.switch(last, shares, here)
    where = jnp.stack([k, jnp.bitwise_xor(k, mask), occ_block * occ_dev, (1 - occ_block) * occ_dev]).astype(jnp.int32)
    return combine(where, occ_energy, vir_energy, own, near, far)[None]


def solution(mesh):
    placed = (P("kv", "occ", None, None), P(), P(), P())
    return jax.shard_map(
        shards, mesh=mesh, in_specs=placed, out_specs=P("kv", "occ", None, None), check_vma=False
    )
```

```python
import functools

import jax
import jax.numpy as jnp
from jax import lax
from jax.experimental import pallas as pl
from jax.experimental.pallas import tpu as pltpu
from jax.sharding import PartitionSpec as P


GROUP = 2


def combine_kernel(ids, partners, occ, vir, own, near, far, out, comb, result, out_sems):
    occ_dev, vir_count, aux = own.shape
    half = occ_dev * vir_count
    k, own_base = ids[0], ids[1]
    q = jnp.bitwise_xor(k, partners[0, 0])
    far_base = ids[2]
    own_vir = jnp.transpose(jnp.broadcast_to(vir[pl.ds(k, 1), :], (vir_count, vir_count)))
    vir_sum = own_vir + vir[pl.ds(q, 1), :]
    own_rows = own[...].reshape(half, aux)

    def mix(numer, first, count):
        for place in range(count):
            j = first + place
            base = own_base + j if j < occ_dev else far_base + j - occ_dev
            there = place * vir_count
            for i in range(occ_dev):
                here = i * vir_count
                den = (occ[k, own_base + i] + occ[q, base]) - vir_sum
                tile = numer[here : here + vir_count, there : there + vir_count]
                direct = (tile / den).astype(jnp.bfloat16).astype(jnp.float32)
                mixed = (2.0 * direct - jnp.transpose(direct)).astype(jnp.bfloat16)
                comb[here : here + vir_count, j * vir_count : (j + 1) * vir_count] = mixed

    def numer(other):
        return lax.dot_general(
            own_rows, other, (((1,), (1,)), ((), ())), preferred_element_type=jnp.float32
        )

    def flat(x):
        return x.reshape(-1, aux)

    mix(numer(flat(near[0:2])), 0, 2)
    mix(numer(flat(jnp.concatenate([near[2:3], far[0:1]]))), 2, 2)
    mix(numer(flat(far[1:3])), 4, 2)
    strips = out_sems.shape[0]
    wide = aux // strips

    def store(strip):
        cols = pl.ds(pl.multiple_of(strip * wide, wide), wide)
        return pltpu.make_async_copy(result.at[:, :, cols], out.at[:, :, cols], out_sems.at[strip])

    def fold(strip, carry):
        cols = pl.ds(pl.multiple_of(strip * wide, wide), wide)
        part = jnp.dot(comb[:, :half], near[:, :, cols].reshape(half, wide), preferred_element_type=jnp.float32)
        part += jnp.dot(comb[:, half:], far[:, :, cols].reshape(half, wide), preferred_element_type=jnp.float32)
        result[:, :, cols] = part.reshape(occ_dev, vir_count, wide)
        store(strip).start()
        return carry

    lax.fori_loop(0, strips, fold, 0, unroll=4)
    for strip in range(strips):
        store(strip).wait()


def combine(ids, partners, occ_energy, vir_energy, own, near, far, strips=4):
    occ_dev, vir_count, aux = own.shape
    half = occ_dev * vir_count
    vmem = pl.BlockSpec(memory_space=pltpu.VMEM)
    smem = pl.BlockSpec(memory_space=pltpu.SMEM)
    return pl.pallas_call(
        combine_kernel,
        out_shape=jax.ShapeDtypeStruct(own.shape, jnp.float32),
        in_specs=[smem, smem, smem, vmem, vmem, vmem, vmem],
        out_specs=pl.BlockSpec(memory_space=pltpu.HBM),
        scratch_shapes=[
            pltpu.VMEM((half, 2 * half), own.dtype),
            pltpu.VMEM(own.shape, jnp.float32),
            pltpu.SemaphoreType.DMA((strips,)),
        ],
        compiler_params=pltpu.CompilerParams(vmem_limit_bytes=24 << 20),
        cost_estimate=pl.CostEstimate(
            flops=8 * half * half * aux, bytes_accessed=10 * half * aux, transcendentals=0
        ),
    )(ids, partners, occ_energy, vir_energy, own, near, far)


def hop(x, mask, side, kv_count, occ_groups):
    pairs = [
        (k * occ_groups + o, (k ^ mask) * occ_groups + (o ^ side))
        for k in range(kv_count)
        for o in range(occ_groups)
    ]
    return lax.ppermute(x, ("kv", "occ"), pairs)


def route(mask, kv_count, occ_groups, own):
    return hop(own, mask, 0, kv_count, occ_groups) if mask else own


def share(mask, kv_count, occ_groups, here):
    top = kv_count // 2
    if mask & top and mask != top:
        here = hop(here, mask - top, 0, kv_count, occ_groups)
        mask = top
    near = hop(here, mask, 0, kv_count, occ_groups) if mask else here
    return near, hop(here, mask, 1, kv_count, occ_groups)


def choose(index, branches, operand):
    if len(branches) <= 16:
        return lax.switch(index, branches, operand)
    half = len(branches) // 2
    return lax.cond(
        index < half,
        lambda x: choose(index, branches[:half], x),
        lambda x: choose(index - half, branches[half:], x),
        operand,
    )


def shards(factors, occ_energy, vir_energy, partners):
    kv_count = lax.axis_size("kv")
    occ_groups = lax.axis_size("occ")
    k = lax.axis_index("kv")
    occ_block = lax.axis_index("occ")
    occ_dev = factors.shape[1]
    own = factors[0]
    top = kv_count // 2

    def routes(masks):
        return [functools.partial(route, m, kv_count, occ_groups) for m in masks]

    ids = jnp.stack([k, occ_block * occ_dev, (1 - occ_block) * occ_dev]).astype(jnp.int32)
    code = kv_count * (k + 1).astype(jnp.int32) + partners[0, 0]
    along = jnp.bitwise_and(jnp.right_shift(code, 1), top // 2 - 1)
    last = jnp.bitwise_and(code, 1) + 2 * jnp.bitwise_and(jnp.right_shift(code, kv_count.bit_length() - 2), 1)
    here = choose(along, routes(range(0, top, 2)), own)
    shares = [functools.partial(share, m, kv_count, occ_groups) for m in (0, 1, top, top + 1)]
    near, far = lax.switch(last, shares, here)
    return combine(ids, partners, occ_energy, vir_energy, own, near, far)[None]


def solution(mesh):
    placed = (P("kv", "occ", None, None), P(), P(), P())
    return jax.shard_map(
        shards, mesh=mesh, in_specs=placed, out_specs=P("kv", "occ", None, None), check_vma=False
    )
```

```python
import functools

import jax
import jax.numpy as jnp
from jax import lax
from jax.experimental import pallas as pl
from jax.experimental.pallas import tpu as pltpu
from jax.sharding import PartitionSpec as P


GROUP = 2


def combine_kernel(ids, occ, vir, own, near, far, out, comb, result, out_sems):
    occ_dev, vir_count, aux = own.shape
    half = occ_dev * vir_count
    k, q, first = ids[0], ids[1], ids[2] == 0
    lane = lax.broadcasted_iota(jnp.int32, occ.shape, 1)

    def column(momentum):
        energy = jnp.sum(jnp.where(lane == momentum, occ[...], 0.0), axis=1, keepdims=True)
        low, high = energy[:occ_dev], energy[occ_dev:]
        return jnp.where(first, low, high), jnp.where(first, high, low)

    own_occ, _ = column(k)
    far_occ = jnp.concatenate(column(q), axis=0)
    own_vir = jnp.transpose(jnp.broadcast_to(vir[pl.ds(k, 1), :], (vir_count, vir_count)))
    vir_sum = own_vir + vir[pl.ds(q, 1), :]
    own_rows = own[...].reshape(half, aux)
    for step in range(2 * occ_dev // GROUP):
        left, right = step * GROUP, (step + 1) * GROUP
        if right <= occ_dev:
            other = near[left:right]
        elif left >= occ_dev:
            other = far[left - occ_dev : right - occ_dev]
        else:
            other = jnp.concatenate([near[left:], far[: right - occ_dev]])
        other = other.reshape(GROUP * vir_count, aux)
        numer = lax.dot_general(
            own_rows, other, (((1,), (1,)), ((), ())), preferred_element_type=jnp.float32
        )
        for place in range(GROUP):
            j = step * GROUP + place
            there = place * vir_count
            for i in range(occ_dev):
                here = i * vir_count
                den = (own_occ[i : i + 1] + far_occ[j : j + 1]) - vir_sum
                tile = numer[here : here + vir_count, there : there + vir_count]
                direct = (tile / den).astype(jnp.bfloat16).astype(jnp.float32)
                mixed = (2.0 * direct - jnp.transpose(direct)).astype(jnp.bfloat16)
                comb[here : here + vir_count, j * vir_count : (j + 1) * vir_count] = mixed
    strips = out_sems.shape[0]
    wide = aux // strips
    stores = []
    for strip in range(strips):
        cols = pl.ds(strip * wide, wide)
        part = jnp.dot(
            comb[:, :half], near[:, :, cols].reshape(half, wide), preferred_element_type=jnp.float32
        )
        part += jnp.dot(
            comb[:, half:], far[:, :, cols].reshape(half, wide), preferred_element_type=jnp.float32
        )
        result[:, :, cols] = part.reshape(occ_dev, vir_count, wide)
        stores.append(pltpu.make_async_copy(result.at[:, :, cols], out.at[:, :, cols], out_sems.at[strip]))
        stores[-1].start()
    for store in stores:
        store.wait()


def combine(ids, occ_energy, vir_energy, own, near, far, strips=4):
    occ_dev, vir_count, aux = own.shape
    half = occ_dev * vir_count
    vmem = pl.BlockSpec(memory_space=pltpu.VMEM)
    smem = pl.BlockSpec(memory_space=pltpu.SMEM)
    return pl.pallas_call(
        combine_kernel,
        out_shape=jax.ShapeDtypeStruct(own.shape, jnp.float32),
        in_specs=[smem, vmem, vmem, vmem, vmem, vmem],
        out_specs=pl.BlockSpec(memory_space=pl.ANY),
        scratch_shapes=[
            pltpu.VMEM((half, 2 * half), own.dtype),
            pltpu.VMEM(own.shape, jnp.float32),
            pltpu.SemaphoreType.DMA((strips,)),
        ],
        compiler_params=pltpu.CompilerParams(vmem_limit_bytes=24 << 20),
        cost_estimate=pl.CostEstimate(
            flops=8 * half * half * aux, bytes_accessed=10 * half * aux, transcendentals=0
        ),
    )(ids, occ_energy.T, vir_energy, own, near, far)


def hop(x, mask, side, kv_count, occ_groups):
    pairs = [
        (k * occ_groups + o, (k ^ mask) * occ_groups + (o ^ side))
        for k in range(kv_count)
        for o in range(occ_groups)
    ]
    return lax.ppermute(x, ("kv", "occ"), pairs)


def route(mask, kv_count, occ_groups, own):
    return hop(own, mask, 0, kv_count, occ_groups) if mask else own


def share(mask, kv_count, occ_groups, here):
    top = kv_count // 2
    if mask & top and mask != top:
        here = hop(here, mask - top, 0, kv_count, occ_groups)
        mask = top
    far = hop(here, mask, 1, kv_count, occ_groups)
    if mask:
        near = hop(here, mask, 0, kv_count, occ_groups)
    else:
        near = here + jnp.minimum(jnp.abs(here), 0)
    return near, far


def choose(index, branches, operand):
    if len(branches) <= 16:
        return lax.switch(index, branches, operand)
    half = len(branches) // 2
    return lax.cond(
        index < half,
        lambda x: choose(index, branches[:half], x),
        lambda x: choose(index - half, branches[half:], x),
        operand,
    )


def shards(factors, occ_energy, vir_energy, partners):
    kv_count = lax.axis_size("kv")
    occ_groups = lax.axis_size("occ")
    k = lax.axis_index("kv")
    occ_block = lax.axis_index("occ")
    occ_dev = factors.shape[1]
    own = factors[0]
    top = kv_count // 2

    def routes(masks):
        return [functools.partial(route, m, kv_count, occ_groups) for m in masks]

    code = kv_count * (k + 1).astype(jnp.int32) + partners[0, 0]
    along = jnp.bitwise_and(jnp.right_shift(code, 1), top // 2 - 1)
    last = jnp.bitwise_and(code, 1) + 2 * jnp.bitwise_and(jnp.right_shift(code, kv_count.bit_length() - 2), 1)
    here = choose(along, routes(range(0, top, 2)), own)
    shares = [functools.partial(share, m, kv_count, occ_groups) for m in (0, 1, top, top + 1)]
    near, far = lax.switch(last, shares, here)
    ids = jnp.stack([k, jnp.bitwise_xor(k, jnp.bitwise_and(code, kv_count - 1)), occ_block]).astype(jnp.int32)
    return combine(ids, occ_energy, vir_energy, own, near, far)[None]


def solution(mesh):
    placed = (P("kv", "occ", None, None), P(), P(), P())
    return jax.shard_map(
        shards, mesh=mesh, in_specs=placed, out_specs=P("kv", "occ", None, None), check_vma=False
    )
```

```python
import functools

import jax
import jax.numpy as jnp
from jax import lax
from jax.experimental import pallas as pl
from jax.experimental.pallas import tpu as pltpu
from jax.sharding import PartitionSpec as P


GROUP = 6


def combine_kernel(ids, occ, vir, own, near, far, out, comb, result, out_sems):
    occ_dev, vir_count, aux = own.shape
    half = occ_dev * vir_count
    k, q, first = ids[0], ids[1], ids[2] == 0
    lane = lax.broadcasted_iota(jnp.int32, occ.shape, 1)

    def column(momentum):
        energy = jnp.sum(jnp.where(lane == momentum, occ[...], 0.0), axis=1, keepdims=True)
        low, high = energy[:occ_dev], energy[occ_dev:]
        return jnp.where(first, low, high), jnp.where(first, high, low)

    own_occ, _ = column(k)
    far_occ = jnp.concatenate(column(q), axis=0)
    own_vir = jnp.transpose(jnp.broadcast_to(vir[pl.ds(k, 1), :], (vir_count, vir_count)))
    vir_sum = own_vir + vir[pl.ds(q, 1), :]
    own_rows = own[...].reshape(half, aux)
    for step in range(2 * occ_dev // GROUP):
        left, right = step * GROUP, (step + 1) * GROUP
        if right <= occ_dev:
            other = near[left:right]
        elif left >= occ_dev:
            other = far[left - occ_dev : right - occ_dev]
        else:
            other = jnp.concatenate([near[left:], far[: right - occ_dev]])
        other = other.reshape(GROUP * vir_count, aux)
        numer = lax.dot_general(
            own_rows, other, (((1,), (1,)), ((), ())), preferred_element_type=jnp.float32
        )
        for place in range(GROUP):
            j = step * GROUP + place
            there = place * vir_count
            for i in range(occ_dev):
                here = i * vir_count
                den = (own_occ[i : i + 1] + far_occ[j : j + 1]) - vir_sum
                tile = numer[here : here + vir_count, there : there + vir_count]
                direct = (tile / den).astype(jnp.bfloat16).astype(jnp.float32)
                mixed = (2.0 * direct - jnp.transpose(direct)).astype(jnp.bfloat16)
                comb[here : here + vir_count, j * vir_count : (j + 1) * vir_count] = mixed
    strips = out_sems.shape[0]
    wide = aux // strips
    stores = []
    for strip in range(strips):
        cols = pl.ds(strip * wide, wide)
        part = jnp.dot(
            comb[:, :half], near[:, :, cols].reshape(half, wide), preferred_element_type=jnp.float32
        )
        part += jnp.dot(
            comb[:, half:], far[:, :, cols].reshape(half, wide), preferred_element_type=jnp.float32
        )
        result[:, :, cols] = part.reshape(occ_dev, vir_count, wide)
        stores.append(pltpu.make_async_copy(result.at[:, :, cols], out.at[:, :, cols], out_sems.at[strip]))
        stores[-1].start()
    for store in stores:
        store.wait()


def combine(ids, occ_energy, vir_energy, own, near, far, strips=4):
    occ_dev, vir_count, aux = own.shape
    half = occ_dev * vir_count
    vmem = pl.BlockSpec(memory_space=pltpu.VMEM)
    smem = pl.BlockSpec(memory_space=pltpu.SMEM)
    return pl.pallas_call(
        combine_kernel,
        out_shape=jax.ShapeDtypeStruct(own.shape, jnp.float32),
        in_specs=[smem, vmem, vmem, vmem, vmem, vmem],
        out_specs=pl.BlockSpec(memory_space=pl.ANY),
        scratch_shapes=[
            pltpu.VMEM((half, 2 * half), own.dtype),
            pltpu.VMEM(own.shape, jnp.float32),
            pltpu.SemaphoreType.DMA((strips,)),
        ],
        compiler_params=pltpu.CompilerParams(vmem_limit_bytes=24 << 20),
        cost_estimate=pl.CostEstimate(
            flops=8 * half * half * aux, bytes_accessed=10 * half * aux, transcendentals=0
        ),
    )(ids, occ_energy.T, vir_energy, own, near, far)


def hop(x, mask, side, kv_count, occ_groups):
    pairs = [
        (k * occ_groups + o, (k ^ mask) * occ_groups + (o ^ side))
        for k in range(kv_count)
        for o in range(occ_groups)
    ]
    return lax.ppermute(x, ("kv", "occ"), pairs)


def route(mask, kv_count, occ_groups, own):
    return hop(own, mask, 0, kv_count, occ_groups) if mask else own


def share(mask, kv_count, occ_groups, here):
    top = kv_count // 2
    if mask & top and mask != top:
        here = hop(here, mask - top, 0, kv_count, occ_groups)
        mask = top
    far = hop(here, mask, 1, kv_count, occ_groups)
    if mask:
        near = hop(here, mask, 0, kv_count, occ_groups)
    else:
        near = here + jnp.minimum(jnp.abs(here), 0)
    return near, far


def choose(index, branches, operand):
    if len(branches) <= 16:
        return lax.switch(index, branches, operand)
    half = len(branches) // 2
    return lax.cond(
        index < half,
        lambda x: choose(index, branches[:half], x),
        lambda x: choose(index - half, branches[half:], x),
        operand,
    )


def shards(factors, occ_energy, vir_energy, partners):
    kv_count = lax.axis_size("kv")
    occ_groups = lax.axis_size("occ")
    k = lax.axis_index("kv")
    occ_block = lax.axis_index("occ")
    occ_dev = factors.shape[1]
    own = factors[0]
    top = kv_count // 2

    def routes(masks):
        return [functools.partial(route, m, kv_count, occ_groups) for m in masks]

    code = kv_count * (k + 1).astype(jnp.int32) + partners[0, 0]
    along = jnp.bitwise_and(jnp.right_shift(code, 1), top // 2 - 1)
    last = jnp.bitwise_and(code, 1) + 2 * jnp.bitwise_and(jnp.right_shift(code, kv_count.bit_length() - 2), 1)
    here = choose(along, routes(range(0, top, 2)), own)
    shares = [functools.partial(share, m, kv_count, occ_groups) for m in (0, 1, top, top + 1)]
    near, far = lax.switch(last, shares, here)
    ids = jnp.stack([k, jnp.bitwise_xor(k, jnp.bitwise_and(code, kv_count - 1)), occ_block]).astype(jnp.int32)
    return combine(ids, occ_energy, vir_energy, own, near, far)[None]


def solution(mesh):
    placed = (P("kv", "occ", None, None), P(), P(), P())
    return jax.shard_map(
        shards, mesh=mesh, in_specs=placed, out_specs=P("kv", "occ", None, None), check_vma=False
    )
```

```python
import functools

import jax
import jax.numpy as jnp
from jax import lax
from jax.experimental import pallas as pl
from jax.experimental.pallas import tpu as pltpu
from jax.sharding import PartitionSpec as P


GROUP = 6


def combine_kernel(ids, occ, vir, own, near, far, out, comb, result, out_sems):
    occ_dev, vir_count, aux = own.shape
    half = occ_dev * vir_count
    k, q, first = ids[0], ids[1], ids[2] == 0
    lane = lax.broadcasted_iota(jnp.int32, occ.shape, 1)

    def column(momentum):
        energy = jnp.sum(jnp.where(lane == momentum, occ[...], 0.0), axis=1, keepdims=True)
        low, high = energy[:occ_dev], energy[occ_dev:]
        return jnp.where(first, low, high), jnp.where(first, high, low)

    own_occ, _ = column(k)
    far_occ = jnp.concatenate(column(q), axis=0)
    own_vir = jnp.transpose(jnp.broadcast_to(vir[pl.ds(k, 1), :], (vir_count, vir_count)))
    vir_sum = own_vir + vir[pl.ds(q, 1), :]
    own_rows = own[...].reshape(half, aux)
    for step in range(2 * occ_dev // GROUP):
        left, right = step * GROUP, (step + 1) * GROUP
        if right <= occ_dev:
            other = near[left:right]
        elif left >= occ_dev:
            other = far[left - occ_dev : right - occ_dev]
        else:
            other = jnp.concatenate([near[left:], far[: right - occ_dev]])
        other = other.reshape(GROUP * vir_count, aux)
        numer = lax.dot_general(
            own_rows, other, (((1,), (1,)), ((), ())), preferred_element_type=jnp.float32
        )
        for place in range(GROUP):
            j = step * GROUP + place
            there = place * vir_count
            for i in range(occ_dev):
                here = i * vir_count
                den = (own_occ[i : i + 1] + far_occ[j : j + 1]) - vir_sum
                tile = numer[here : here + vir_count, there : there + vir_count]
                direct = (tile / den).astype(jnp.bfloat16).astype(jnp.float32)
                mixed = (2.0 * direct - jnp.transpose(direct)).astype(jnp.bfloat16)
                comb[here : here + vir_count, j * vir_count : (j + 1) * vir_count] = mixed
    strips = out_sems.shape[0]
    wide = aux // strips
    stores = []
    for strip in range(strips):
        cols = pl.ds(strip * wide, wide)
        part = jnp.dot(
            comb[:, :half], near[:, :, cols].reshape(half, wide), preferred_element_type=jnp.float32
        )
        part += jnp.dot(
            comb[:, half:], far[:, :, cols].reshape(half, wide), preferred_element_type=jnp.float32
        )
        result[:, :, cols] = part.reshape(occ_dev, vir_count, wide)
        stores.append(pltpu.make_async_copy(result.at[:, :, cols], out.at[:, :, cols], out_sems.at[strip]))
        stores[-1].start(priority=strip % 2)
    for store in stores:
        store.wait()


def combine(ids, occ_energy, vir_energy, own, near, far, strips=4):
    occ_dev, vir_count, aux = own.shape
    half = occ_dev * vir_count
    vmem = pl.BlockSpec(memory_space=pltpu.VMEM)
    smem = pl.BlockSpec(memory_space=pltpu.SMEM)
    return pl.pallas_call(
        combine_kernel,
        out_shape=jax.ShapeDtypeStruct(own.shape, jnp.float32),
        in_specs=[smem, vmem, vmem, vmem, vmem, vmem],
        out_specs=pl.BlockSpec(memory_space=pl.ANY),
        scratch_shapes=[
            pltpu.VMEM((half, 2 * half), own.dtype),
            pltpu.VMEM(own.shape, jnp.float32),
            pltpu.SemaphoreType.DMA((strips,)),
        ],
        compiler_params=pltpu.CompilerParams(vmem_limit_bytes=24 << 20),
        cost_estimate=pl.CostEstimate(
            flops=8 * half * half * aux, bytes_accessed=10 * half * aux, transcendentals=0
        ),
    )(ids, occ_energy.T, vir_energy, own, near, far)


def hop(x, mask, side, kv_count, occ_groups):
    pairs = [
        (k * occ_groups + o, (k ^ mask) * occ_groups + (o ^ side))
        for k in range(kv_count)
        for o in range(occ_groups)
    ]
    return lax.ppermute(x, ("kv", "occ"), pairs)


def route(mask, kv_count, occ_groups, own):
    return hop(own, mask, 0, kv_count, occ_groups) if mask else own


def share(mask, kv_count, occ_groups, here):
    top = kv_count // 2
    if mask & top and mask != top:
        here = hop(here, mask - top, 0, kv_count, occ_groups)
        mask = top
    far = hop(here, mask, 1, kv_count, occ_groups)
    if mask:
        near = hop(here, mask, 0, kv_count, occ_groups)
    else:
        near = here + jnp.minimum(jnp.abs(here), 0)
    return near, far


def choose(index, branches, operand):
    if len(branches) <= 16:
        return lax.switch(index, branches, operand)
    half = len(branches) // 2
    return lax.cond(
        index < half,
        lambda x: choose(index, branches[:half], x),
        lambda x: choose(index - half, branches[half:], x),
        operand,
    )


def shards(factors, occ_energy, vir_energy, partners):
    kv_count = lax.axis_size("kv")
    occ_groups = lax.axis_size("occ")
    k = lax.axis_index("kv")
    occ_block = lax.axis_index("occ")
    occ_dev = factors.shape[1]
    own = factors[0]
    top = kv_count // 2

    def routes(masks):
        return [functools.partial(route, m, kv_count, occ_groups) for m in masks]

    code = kv_count * (k + 1).astype(jnp.int32) + partners[0, 0]
    along = jnp.bitwise_and(jnp.right_shift(code, 1), top // 2 - 1)
    last = jnp.bitwise_and(code, 1) + 2 * jnp.bitwise_and(jnp.right_shift(code, kv_count.bit_length() - 2), 1)
    here = choose(along, routes(range(0, top, 2)), own)
    shares = [functools.partial(share, m, kv_count, occ_groups) for m in (0, 1, top, top + 1)]
    near, far = lax.switch(last, shares, here)
    ids = jnp.stack([k, jnp.bitwise_xor(k, jnp.bitwise_and(code, kv_count - 1)), occ_block]).astype(jnp.int32)
    return combine(ids, occ_energy, vir_energy, own, near, far)[None]


def solution(mesh):
    placed = (P("kv", "occ", None, None), P(), P(), P())
    return jax.shard_map(
        shards, mesh=mesh, in_specs=placed, out_specs=P("kv", "occ", None, None), check_vma=False
    )
```
